256 devices in a mesh: lat: 16 (over z, x_lo), lon: 16 (over y, x_hi, core).
Axes of the slice: x: 4 (x_hi: 2, x_lo: 2; x = x_hi * 2 + x_lo), y: 4, z: 8, core: 2. Of those that a mesh axis runs over, the one named last changes fastest.
Arguments:
- anomalies: bfloat16 [32, 64, 64, 256], P('lat', 'lon'), may hold values from -6 to 6
- innovations: bfloat16 [32, 64, 64, 256], P('lat', 'lon'), may hold values from -1.1953125 to 1.1953125
- taper_table: bfloat16 [16, 256, 256], replicated, may hold values from 0 to 1, as said below
- pair_own: int32 [16, 16, 200], P('lat', 'lon'), may hold values from 0 to 7, as said below
- pair_window: int32 [16, 16, 200], P('lat', 'lon'), may hold values from 0 to 47, as said below
- pair_taper: int32 [16, 16, 200], P('lat', 'lon'), may hold values from 0 to 15, as said below
- pair_owner: int32 [16, 16, 200], P('lat', 'lon'), may hold values from 0 to 1, as said below
- pair_count: int32 [16, 16], P('lat', 'lon'), may hold values from 8 to 200, as said below
Outputs:
- inflated: float32 [32, 64, 64, 256], P('lat', 'lon')
The draws below stay inside these ranges and needn't reach their ends.
Inputs may be any that keep to these rules, and one draw needn't show every extreme that they name: Slots 0 to pair_count - 1 of a device are live; the later slots hold zeros in every pair list. Some device is full in every draw. `pair_own`: A live slot names each of the device's blocks as own block. `pair_window`: A live slot never names a window block beyond the poles, and each (own block, window block) pair stands once. `pair_owner`: for every live slot (a, b) other than a diagonal one (b the window position of a itself), the device of b holds a live mirror slot (b, a); the owner values of a slot and its mirror sum to one; a diagonal slot has owner 1 and no mirror. `pair_taper`: A mirror slot's taper index is its slot's index plus 8, modulo 2 * 8. `taper_table`: entry k + 8 is the transpose of entry k.
All inputs are finite; a program needn't handle non-finite values.
Results may differ from the reference program's by a relative error of at most 0.0033.
Values may be sent and summed in bfloat16 or wider, within the bound.
No kernel may reach another device: no remote copies, remote signals or barrier semaphores. Data moves between devices by JAX's collectives and lax.ppermute only.
A program may use at most 64 MiB of HBM per device.

```python
import jax
import jax.numpy as jnp
from jax import lax

MEMBERS = 64
BLOCK = 256
BANDS_DEV = 2
LONS_DEV = 4
REACH = 2
TAPERS = 8
GROUP = 8
PAIRS = 200
BANDS = 32
LONS = 64
WIN_LAT = 6
WIN_LON = 8
N_LAT = 16
N_LON = 16


def pair_tables(key):
    base = jax.random.fold_in(key, 11)
    key_reach, key_coin, key_taper, key_order = jax.random.split(base, 4)
    offsets = 2 * REACH + 1
    band_list = jnp.arange(BANDS, dtype=jnp.int32)
    reach_draw = jax.random.randint(key_reach, (BANDS,), 0, REACH + 1, dtype=jnp.int32)
    forced = (band_list <= 2 * BANDS_DEV - 1 + REACH) | (band_list >= BANDS - 2 * BANDS_DEV - REACH)
    band_reach = jnp.where(forced, REACH, reach_draw)
    shape = (BANDS, LONS, offsets, offsets)
    band_grid = jnp.broadcast_to(jnp.arange(BANDS, dtype=jnp.int32)[:, None, None, None], shape)
    lon_grid = jnp.broadcast_to(jnp.arange(LONS, dtype=jnp.int32)[None, :, None, None], shape)
    lat_step = jnp.broadcast_to(jnp.arange(offsets, dtype=jnp.int32)[None, None, :, None], shape)
    lon_step = jnp.broadcast_to(jnp.arange(offsets, dtype=jnp.int32)[None, None, None, :], shape)
    other_band = band_grid + lat_step - REACH
    other_lon = (lon_grid + lon_step - REACH) % LONS
    inside = (other_band >= 0) & (other_band < BANDS)
    other_clip = jnp.clip(other_band, 0, BANDS - 1)
    is_live = inside & (jnp.abs(lon_step - REACH) <= jnp.minimum(band_reach[band_grid], band_reach[other_clip]))
    band_coin = jax.random.randint(key_coin, (BANDS,), 0, 2, dtype=jnp.int32)
    coin_flips = (lon_grid + lon_step + band_coin[band_grid]) % 2
    taper_draw = jax.random.randint(key_taper, shape, 0, 2 * TAPERS, dtype=jnp.int32)
    mirror_lat = offsets - 1 - lat_step
    mirror_lon = offsets - 1 - lon_step
    mirror_coin = coin_flips[other_clip, other_lon, mirror_lat, mirror_lon]
    mirror_taper = taper_draw[other_clip, other_lon, mirror_lat, mirror_lon]
    self_ident = band_grid * LONS + lon_grid
    other_ident = other_clip * LONS + other_lon
    canonical = self_ident <= other_ident
    coin_final = jnp.where(canonical, coin_flips, 1 - mirror_coin)
    taper_final = jnp.where(canonical, taper_draw, (mirror_taper + TAPERS) % (2 * TAPERS))
    is_diagonal = (lat_step == REACH) & (lon_step == REACH)
    owner_final = jnp.where(is_diagonal, 1, coin_final)
    local_band = band_grid % BANDS_DEV
    local_lon = lon_grid % LONS_DEV
    own_final = local_band * LONS_DEV + local_lon
    window_final = (local_band + lat_step) * (LONS_DEV + 2 * REACH) + local_lon + lon_step
    lat_devices = BANDS // BANDS_DEV
    lon_devices = LONS // LONS_DEV

    def per_device(values):
        values = values.reshape(lat_devices, BANDS_DEV, lon_devices, LONS_DEV, offsets, offsets)
        values = jnp.transpose(values, (0, 2, 1, 3, 4, 5))
        return values.reshape(lat_devices, lon_devices, PAIRS)
    live_int = per_device(is_live.astype(jnp.int32))
    noise = jax.random.randint(key_order, (lat_devices, lon_devices, PAIRS), 0, PAIRS, dtype=jnp.int32)
    slot_iota = jnp.arange(PAIRS, dtype=jnp.int32)[None, None, :]
    score = (1 - live_int) * (PAIRS * PAIRS) + noise * PAIRS + slot_iota
    ordering = jnp.argsort(score, axis=-1)

    def arrange(values):
        return jnp.take_along_axis(per_device(values), ordering, axis=-1)
    live_sorted = jnp.take_along_axis(live_int, ordering, axis=-1)
    own_out = arrange(own_final) * live_sorted
    window_out = arrange(window_final) * live_sorted
    taper_out = arrange(taper_final) * live_sorted
    owner_out = arrange(owner_final) * live_sorted
    count_out = jnp.sum(live_int, axis=-1).astype(jnp.int32)
    return (own_out, window_out, taper_out, owner_out, count_out)


def draw_pair_own(key, part):
    return pair_tables(key)[0]


def draw_pair_window(key, part):
    return pair_tables(key)[1]


def draw_pair_taper(key, part):
    return pair_tables(key)[2]


def draw_pair_owner(key, part):
    return pair_tables(key)[3]


def draw_pair_count(key, part):
    return pair_tables(key)[4]


def draw_taper_table(key, part):
    tiles = jax.random.uniform(key, (TAPERS, BLOCK, BLOCK), jnp.float32, 0.2, 1.0)
    return jnp.concatenate([tiles, jnp.swapaxes(tiles, 1, 2)], axis=0).astype(jnp.bfloat16)


def level_of(stream_key, extent, cuts, smallest, high):
    loudness = 1.0
    for position, shards_of in cuts:
        steps = jax.random.uniform(jax.random.fold_in(jax.random.fold_in(stream_key, 6), position), (shards_of,), jnp.float32, smallest / len(cuts), high / len(cuts))
        loudness = loudness * jnp.repeat(jnp.exp(steps), extent[position] // shards_of).reshape((-1,) + (1,) * (len(extent) - 1 - position))
    return loudness


def scatter_about(key, shape, deviation, reach, shards=(), kind=jnp.bfloat16):
    result = deviation * jax.random.normal(key, shape, jnp.float32)
    if shards:
        result = result * level_of(key, shape, shards, -0.22, 0.18)
    return jnp.clip(result, -reach, reach).astype(kind)


def setup_inputs(seed: int = 0) -> dict:
    keys = jax.random.split(jax.random.key(seed), 9)
    anomalies = scatter_about(keys[0], (BANDS, LONS, MEMBERS, BLOCK), 1.0, 6.0, ((0, 16), (1, 16)))
    innovations = scatter_about(keys[1], (BANDS, LONS, MEMBERS, BLOCK), 0.2, 1.1953125, ((0, 16), (1, 16)))
    taper_table = draw_taper_table(jax.random.fold_in(keys[8], 71), 0)
    pair_own = draw_pair_own(jax.random.fold_in(keys[8], 71), 0)
    pair_window = draw_pair_window(jax.random.fold_in(keys[8], 71), 0)
    pair_taper = draw_pair_taper(jax.random.fold_in(keys[8], 71), 0)
    pair_owner = draw_pair_owner(jax.random.fold_in(keys[8], 71), 0)
    pair_count = draw_pair_count(jax.random.fold_in(keys[8], 71), 0)
    return {"anomalies": anomalies, "innovations": innovations, "taper_table": taper_table, "pair_own": pair_own, "pair_window": pair_window, "pair_taper": pair_taper, "pair_owner": pair_owner, "pair_count": pair_count}


def reference(anomalies, innovations, taper_table, pair_own, pair_window, pair_taper, pair_owner, pair_count):
    padding = ((REACH, REACH), (0, 0), (0, 0), (0, 0))
    anom_padded = jnp.pad(anomalies, padding)
    innov_padded = jnp.pad(innovations, padding)
    home_count = BANDS_DEV * LONS_DEV
    window_count = WIN_LAT * WIN_LON
    slot_iota = jnp.arange(PAIRS, dtype=jnp.int32)
    lat_iota = jnp.arange(WIN_LAT, dtype=jnp.int32)
    lon_iota = jnp.arange(WIN_LON, dtype=jnp.int32)
    group_iota = jnp.arange(GROUP, dtype=jnp.int32)

    def one_device(accumulated, device):
        lat_device = device // N_LON
        lon_device = device % N_LON
        lon_index = ((lon_device * LONS_DEV - REACH + lon_iota) % LONS).astype(jnp.int32)
        start_row = (lat_device * BANDS_DEV).astype(jnp.int32)
        window_anom = jnp.take(lax.dynamic_slice_in_dim(anom_padded, start_row, WIN_LAT, 0), lon_index, axis=1)
        window_innov = jnp.take(lax.dynamic_slice_in_dim(innov_padded, start_row, WIN_LAT, 0), lon_index, axis=1)
        home_anom = window_anom[REACH:REACH + BANDS_DEV, REACH:REACH + LONS_DEV].reshape(home_count, MEMBERS, BLOCK)
        home_innov = window_innov[REACH:REACH + BANDS_DEV, REACH:REACH + LONS_DEV].reshape(home_count, MEMBERS, BLOCK)
        window_anom = window_anom.reshape(window_count, MEMBERS, BLOCK)
        window_innov = window_innov.reshape(window_count, MEMBERS, BLOCK)
        live_count = pair_count[lat_device, lon_device]
        wanted = (slot_iota < live_count) & (pair_owner[lat_device, lon_device] == 1)
        ordering = jnp.argsort(jnp.where(wanted, 0, PAIRS).astype(jnp.int32) + slot_iota)
        home_index = pair_own[lat_device, lon_device][ordering]
        window_index = pair_window[lat_device, lon_device][ordering]
        taper_index = pair_taper[lat_device, lon_device][ordering]
        wanted_total = jnp.sum(wanted.astype(jnp.int32))
        group_trips = (wanted_total + GROUP - 1) // GROUP

        def one_group(group_step, partial_value):
            first_slot = (group_step * GROUP).astype(jnp.int32)
            home_part = lax.dynamic_slice_in_dim(home_index, first_slot, GROUP)
            window_part = lax.dynamic_slice_in_dim(window_index, first_slot, GROUP)
            taper_part = lax.dynamic_slice_in_dim(taper_index, first_slot, GROUP)
            weight = (first_slot + group_iota < wanted_total).astype(jnp.float32)
            anom_home = jnp.take(home_anom, home_part, axis=0).astype(jnp.float32)
            anom_window = jnp.take(window_anom, window_part, axis=0).astype(jnp.float32)
            product = jnp.einsum('gkx,gky->gxy', anom_home, anom_window)
            tapers = jnp.take(taper_table, taper_part, axis=0).astype(jnp.float32)
            covariance = (product / (MEMBERS - 1) * tapers).astype(jnp.bfloat16).astype(jnp.float32)
            innov_window = jnp.take(window_innov, window_part, axis=0).astype(jnp.float32)
            innov_home = jnp.take(home_innov, home_part, axis=0).astype(jnp.float32)
            to_home = jnp.einsum('gmy,gxy->gmx', innov_window, covariance)
            to_window = jnp.einsum('gmx,gxy->gmy', innov_home, covariance)
            home_slot = ((home_part // LONS_DEV + REACH) * WIN_LON + home_part % LONS_DEV + REACH).astype(jnp.int32)
            diagonal = (home_slot == window_part).astype(jnp.float32)
            partial_value = partial_value.at[home_slot].add(to_home * weight[:, None, None])
            return partial_value.at[window_part].add(to_window * (weight * (1.0 - diagonal))[:, None, None])
        partial_value = lax.fori_loop(0, group_trips, one_group, jnp.zeros((window_count, MEMBERS, BLOCK), jnp.float32))
        lat_index = (start_row + lat_iota).astype(jnp.int32)
        accumulated = accumulated.at[lat_index[:, None], lon_index[None, :]].add(partial_value.reshape(WIN_LAT, WIN_LON, MEMBERS, BLOCK))
        return (accumulated, None)
    accumulated = jnp.zeros((BANDS + 2 * REACH, LONS, MEMBERS, BLOCK), jnp.float32)
    accumulated, _ = lax.scan(one_device, accumulated, jnp.arange(N_LAT * N_LON, dtype=jnp.int32))
    increment = accumulated[REACH:REACH + BANDS]
    prior = anomalies.astype(jnp.float32)
    posterior = prior - increment
    prior_spread = jnp.sqrt(lax.optimization_barrier(jnp.sum(prior * prior, axis=2)) / (MEMBERS - 1))
    posterior_spread = jnp.sqrt(lax.optimization_barrier(jnp.sum(posterior * posterior, axis=2)) / (MEMBERS - 1) + 1e-06)
    factor = 0.7 * prior_spread / posterior_spread + 0.3
    return posterior * factor[:, :, None, :]
```

```python
import functools

import jax
import jax.numpy as jnp
from jax import lax
from jax.experimental import pallas as pl
from jax.experimental.pallas import tpu as pltpu
from jax.sharding import PartitionSpec as P

MEMBERS = 64
BLOCK = 256
REACH = 2
UNROLL = 16
LIST = 256
SLOTS = 200
COUNTS = 4 * LIST
VMEM_LIMIT = 24 * 2**20
F32 = jnp.float32
BF16 = jnp.bfloat16


def permuted(value, target):
    bands, lons = (lax.axis_size("lat"), lax.axis_size("lon"))
    pairs = []
    for i in range(bands):
        for j in range(lons):
            a, b = target(i, j)
            if 0 <= a < bands:
                pairs.append((i * lons + j, a * lons + b % lons))
    return lax.ppermute(value, ("lat", "lon"), pairs)


def to_partner(i, j):
    return (i ^ 1, j)


def to_beyond(i, j):
    return (i + 2 if i % 2 == 0 else i - 2, j)


def to_diagonal(i, j):
    return (i ^ 1, j + 1 if j % 2 else j - 1)


def to_other_core(i, j):
    return (i, j ^ 1)


def slot_entries(own, window, taper):
    row, lon = (window // 8, window % 8)
    odd_lat = lax.axis_index("lat") % 2
    odd_lon = lax.axis_index("lon") % 2
    partner_row = jnp.where(odd_lat == 1, 0, 2)
    rows = row // 2
    group = jnp.where(rows == 1, 0, jnp.where(rows == partner_row, 1, 2))
    west = lon < REACH
    east = lon >= 8 - REACH
    outer = jnp.where(odd_lon == 1, east, west)
    side = west | east
    center_slot = (row % 2) * 4 + lon - REACH
    side_slot = (row % 2) * 2 + jnp.where(west, lon, lon - 6)
    center_phase = group
    outer_phase = jnp.where(group == 1, 1, 2)
    outer_first = jnp.where(group == 0, 8, jnp.where(group == 1, 12, 16))
    inner_phase = group + 1
    inner_first = jnp.where(group == 0, 8, jnp.where(group == 1, 12, 0))
    phase = jnp.where(side, jnp.where(outer, outer_phase, inner_phase), center_phase)
    slot = jnp.where(
        side, jnp.where(outer, outer_first, inner_first) + side_slot, center_slot
    )
    return own + slot * 16 + taper * 1024 + phase * 16384


def pairs_of(lists, phase, home, window_anom, window_innov, tapers, total):
    def group(step, carry):
        for lane in range(UNROLL):
            entry = lists[phase * LIST + step * UNROLL + lane]
            own = entry & 15
            slot = (entry >> 4) & 63
            taper = (entry >> 10) & 15
            product = lax.dot_general(
                home[own & 7],
                window_anom[slot],
                (((0,), (0,)), ((), ())),
                preferred_element_type=F32,
            )
            tile = (product * tapers[taper].astype(F32)).astype(BF16)
            total[own] += lax.dot_general(
                tile, window_innov[slot], (((1,), (1,)), ((), ())), preferred_element_type=F32
            )
        return carry

    count = lists[COUNTS + phase]
    lax.fori_loop(0, (count + UNROLL - 1) // UNROLL, group, 0)


def first_kernel(entries, home, innov, tapers, total, lists):
    for phase in range(4):
        lists[COUNTS + phase] = 0

    def place(s, carry):
        entry = entries[s]
        phase = entry >> 14
        position = lists[COUNTS + phase]
        lists[phase * LIST + position] = entry & 16383
        lists[COUNTS + phase] = position + 1
        return carry

    lax.fori_loop(0, entries[SLOTS], place, 0)
    for phase in range(4):
        position = lists[COUNTS + phase]
        for lane in range(UNROLL):
            lists[phase * LIST + position + lane] = 8
    total[...] = jnp.zeros_like(total)
    pairs_of(lists, 0, home, home, innov, tapers, total)


def gathered(parts, sides, anom, innov):
    first = 0
    if parts is not None:
        anom[0:8] = parts[0][...]
        innov[0:8] = parts[1][...]
        first = 8
    for side in sides:
        anom[first : first + 4] = side[0]
        innov[first : first + 4] = side[1]
        first += 4


def middle_kernel(phase, lists, home, tapers, before, near_anom, near_innov, *rest):
    sides, (total, anom, innov) = (rest[:-3], rest[-3:])
    gathered((near_anom, near_innov), sides, anom, innov)
    total[...] = before[...]
    pairs_of(lists, phase, home, anom, innov, tapers, total)


def last_kernel(lists, home, tapers, before, side, out, total, anom, innov):
    gathered(None, (side,), anom, innov)
    total[...] = before[...]
    pairs_of(lists, 3, home, anom, innov, tapers, total)
    for own in range(8):
        prior = home[own].astype(F32)
        posterior = prior - total[own].T * (1.0 / (MEMBERS - 1))
        prior_spread = jnp.sqrt(jnp.sum(prior * prior, axis=0, keepdims=True) / (MEMBERS - 1))
        posterior_spread = jnp.sqrt(
            jnp.sum(posterior * posterior, axis=0, keepdims=True) / (MEMBERS - 1) + 1e-06
        )
        out[own] = posterior * (0.7 * prior_spread / posterior_spread + 0.3)


SMEM = pl.BlockSpec(memory_space=pltpu.SMEM)
VMEM = pl.BlockSpec(memory_space=pltpu.VMEM)
TOTAL = jax.ShapeDtypeStruct((9, BLOCK, MEMBERS), F32)


def called(kernel, name, specs, out_shape, out_specs, scratch, pairs):
    return pl.pallas_call(
        kernel,
        in_specs=specs,
        out_shape=out_shape,
        out_specs=out_specs,
        scratch_shapes=scratch,
        compiler_params=pltpu.CompilerParams(vmem_limit_bytes=VMEM_LIMIT),
        cost_estimate=pl.CostEstimate(
            flops=pairs * 8 * MEMBERS * BLOCK * BLOCK * 4, bytes_accessed=4 * 2**20, transcendentals=0
        ),
        name=name,
    )


def local(
    anomalies, innovations, taper_table, pair_own, pair_window, pair_taper, pair_owner, pair_count
):
    odd_lon = lax.axis_index("lon") % 2

    def outer(value):
        return jnp.where(odd_lon == 1, value[:, REACH:], value[:, :REACH])

    def inner(value):
        return jnp.where(odd_lon == 1, value[:, :REACH], value[:, REACH:])

    def both(part, first, second):
        return jnp.stack([part(first), part(second)])

    def flat(value):
        return value.reshape(8, MEMBERS, BLOCK)

    def flat_side(value):
        return value.reshape(2, 4, MEMBERS, BLOCK)

    partner = [permuted(v, to_partner) for v in (anomalies, innovations)]
    partner_outer = permuted(both(outer, anomalies, innovations), to_diagonal)
    home_inner = permuted(both(inner, anomalies, innovations), to_other_core)
    beyond = [permuted(v, to_beyond) for v in partner]
    home_outer = permuted(both(outer, *partner), to_diagonal)
    beyond_outer = permuted(partner_outer, to_beyond)
    partner_inner = permuted(both(inner, *partner), to_other_core)
    beyond_inner = permuted(both(inner, *beyond), to_other_core)

    entries = slot_entries(
        pair_own.reshape(-1), pair_window.reshape(-1), pair_taper.reshape(-1)
    )
    entries = jnp.concatenate([entries, pair_count.reshape(1), jnp.zeros((55,), jnp.int32)])
    home = flat(anomalies)
    scratch = lambda count: [pltpu.VMEM((count, MEMBERS, BLOCK), BF16)] * 2

    total, lists = called(
        first_kernel,
        "home_pairs",
        [SMEM, VMEM, VMEM, VMEM],
        (TOTAL, jax.ShapeDtypeStruct((COUNTS + 8,), jnp.int32)),
        (VMEM, SMEM),
        [],
        56,
    )(entries, home, flat(innovations), taper_table)
    total = called(
        functools.partial(middle_kernel, 1),
        "partner_pairs",
        [SMEM] + [VMEM] * 7,
        TOTAL,
        VMEM,
        scratch(16),
        63,
    )(
        lists,
        home,
        taper_table,
        total,
        flat(partner[0]),
        flat(partner[1]),
        flat_side(home_inner),
        flat_side(partner_outer),
    )
    total = called(
        functools.partial(middle_kernel, 2),
        "beyond_pairs",
        [SMEM] + [VMEM] * 8,
        TOTAL,
        VMEM,
        scratch(20),
        72,
    )(
        lists,
        home,
        taper_table,
        total,
        flat(beyond[0]),
        flat(beyond[1]),
        flat_side(home_outer),
        flat_side(partner_inner),
        flat_side(beyond_outer),
    )
    out = called(
        last_kernel,
        "inflation",
        [SMEM] + [VMEM] * 4,
        jax.ShapeDtypeStruct((8, MEMBERS, BLOCK), F32),
        VMEM,
        [pltpu.VMEM((9, BLOCK, MEMBERS), F32)] + scratch(4),
        9,
    )(lists, home, taper_table, total, flat_side(beyond_inner))
    return out.reshape(anomalies.shape)


def solution(mesh):
    placed = (
        P("lat", "lon", None, None),
        P("lat", "lon", None, None),
        P(),
        P("lat", "lon", None),
        P("lat", "lon", None),
        P("lat", "lon", None),
        P("lat", "lon", None),
        P("lat", "lon"),
    )
    return jax.shard_map(
        local, mesh=mesh, in_specs=placed, out_specs=P("lat", "lon", None, None), check_vma=False
    )
```

```python
import functools

import jax
import jax.numpy as jnp
from jax import lax
from jax.experimental import pallas as pl
from jax.experimental.pallas import tpu as pltpu
from jax.sharding import PartitionSpec as P

MEMBERS = 64
BLOCK = 256
REACH = 2
UNROLL = 4
LIST = 264
SLOTS = 200
PHASES = 5
COUNTS = (PHASES + 1) * LIST
VMEM_LIMIT = 8 * 2**20
F32 = jnp.float32
BF16 = jnp.bfloat16


def permuted(value, target):
    bands, lons = (lax.axis_size("lat"), lax.axis_size("lon"))
    pairs = []
    for i in range(bands):
        for j in range(lons):
            a, b = target(i, j)
            pairs.append((i * lons + j, a * lons + b % lons))
    return lax.ppermute(value, ("lat", "lon"), pairs)


def to_partner(i, j):
    return (i ^ 1, j)


def to_beyond(i, j):
    last = lax.axis_size("lat") - 1
    target = i + 2 if i % 2 == 0 else i - 2
    return (target if 0 <= target <= last else i ^ 1, j)


def to_far_diagonal(i, j):
    last = lax.axis_size("lat") - 1
    target = i + 1 if i % 2 else i - 1
    return (target if 0 <= target <= last else i, j + 1 if j % 2 else j - 1)


def to_diagonal(i, j):
    return (i ^ 1, j + 1 if j % 2 else j - 1)


def to_other_core(i, j):
    return (i, j ^ 1)


def slot_entries(own, window, taper, count):
    row, lon = (window // 8, window % 8)
    odd_lat = lax.axis_index("lat") % 2
    odd_lon = lax.axis_index("lon") % 2
    partner_row = jnp.where(odd_lat == 1, 0, 2)
    rows = row // 2
    group = jnp.where(rows == 1, 0, jnp.where(rows == partner_row, 1, 2))
    west = lon < REACH
    east = lon >= 8 - REACH
    outer = jnp.where(odd_lon == 1, east, west)
    side = west | east
    center_slot = (row % 2) * 4 + lon - REACH
    side_slot = (row % 2) * 2 + jnp.where(west, lon, lon - 6)
    outer_phase = jnp.where(group == 1, 1, 2)
    outer_first = jnp.where(group == 0, 4, jnp.where(group == 1, 12, 8))
    inner_phase = jnp.where(group == 2, 4, group + 1)
    inner_first = jnp.where(group == 0, 8, 0)
    center_phase = jnp.where(group == 2, 3, group)
    phase = jnp.where(side, jnp.where(outer, outer_phase, inner_phase), center_phase)
    slot = jnp.where(
        side, jnp.where(outer, outer_first, inner_first) + side_slot, center_slot
    )
    live = jnp.arange(SLOTS, dtype=jnp.int32) < count
    phase = jnp.where(live, phase, PHASES)
    padding = jnp.arange(LIST - SLOTS, dtype=jnp.int32)
    entries = jnp.concatenate(
        [own + slot * 16 + (taper + 8) % 16 * 1024, jnp.full((LIST - SLOTS,), 8, jnp.int32)]
    )
    phases = jnp.concatenate([phase, jnp.minimum(padding // (3 * UNROLL), PHASES)])
    index = jnp.arange(LIST, dtype=jnp.int32)
    earlier = (phases[:, None] == phases[None, :]) & (index[:, None] < index[None, :])
    place = jnp.sum(earlier.astype(jnp.int32), axis=0)
    return entries + (phases * LIST + place) * 16384


def pairs_of(lists, phase, home, window_anom, window_innov, tapers, total, even, odd):
    def entry_at(group, lane):
        return lists[phase * LIST + group * UNROLL + lane]

    def tiles(group, kept):
        for lane in range(UNROLL):
            entry = entry_at(group, lane)
            product = lax.dot_general(
                window_anom[(entry >> 4) & 63],
                home[entry & 7],
                (((0,), (0,)), ((), ())),
                preferred_element_type=F32,
            )
            kept[lane] = (product * tapers[(entry >> 10) & 15].astype(F32)).astype(BF16)

    def increments(group, kept):
        for lane in range(UNROLL):
            entry = entry_at(group, lane)
            total[entry & 15] += jnp.dot(
                window_innov[(entry >> 4) & 63], kept[lane], preferred_element_type=F32
            )

    def two_groups(step, carry):
        tiles(2 * step + 1, odd)
        increments(2 * step, even)
        tiles(2 * step + 2, even)
        increments(2 * step + 1, odd)
        return carry

    tiles(0, even)
    groups = (lists[COUNTS + phase] + UNROLL - 1) // UNROLL
    lax.fori_loop(0, (groups + 1) // 2, two_groups, 0)


def side_kernel(anom, innov, after, *rest):
    *sides, done = rest
    first = 2 * (lax.axis_index("lon") % 2)
    copies = []
    for place, side in zip((2 - first, first), sides):
        for part, value in ((0, anom), (1, innov)):
            copies.append(
                pltpu.make_async_copy(
                    value.at[:, pl.ds(place, REACH)], side.at[part], done.at[len(copies)]
                )
            )
    for copy in copies:
        copy.start()
    for copy in copies:
        copy.wait()


def first_kernel(entries, *refs):
    sources, (total, lists, even, odd, home, innov, tapers, done) = (refs[:3], refs[3:])
    copies = [
        pltpu.make_async_copy(source, target, done.at[i])
        for i, (source, target) in enumerate(zip(sources, (home, innov, tapers)))
    ]
    for copy in copies:
        copy.start()

    def place(step, carry):
        for lane in range(8):
            entry = entries[step * 8 + lane]
            lists[entry >> 14] = entry & 16383
        return carry

    lax.fori_loop(0, LIST // 8, place, 0)
    for phase in range(PHASES):
        first = entries[SLOTS + 3 * UNROLL * phase] >> 14
        lists[COUNTS + phase] = first - phase * LIST
    total[...] = jnp.zeros_like(total)
    for copy in copies:
        copy.wait()
    pairs_of(lists, 0, home, home, innov, tapers, total, even, odd)


def gathered(parts, sides, anom, innov):
    first = 0
    if parts is not None:
        anom[0:8] = parts[0][...]
        innov[0:8] = parts[1][...]
        first = 8
    for side in sides:
        anom[first : first + 4] = side[0]
        innov[first : first + 4] = side[1]
        first += 4


def middle_kernel(phase, centers, lists, home, tapers, *rest):
    parts, (total, anom, innov, even, odd) = (rest[:-5], rest[-5:])
    gathered(parts[:2] if centers else None, parts[2:] if centers else parts, anom, innov)
    total[...] = jnp.zeros_like(total)
    pairs_of(lists, phase, home, anom, innov, tapers, total, even, odd)


def last_kernel(lists, home, tapers, side, *rest):
    before, (out, total, anom, innov, even, odd) = (rest[:-6], rest[-6:])
    gathered(None, (side,), anom, innov)
    total[...] = jnp.zeros_like(total)
    pairs_of(lists, 4, home, anom, innov, tapers, total, even, odd)
    for own in range(8):
        prior = home[own].astype(F32)
        increment = total[own]
        for part in before:
            increment += part[own]
        posterior = prior - increment * (1.0 / (MEMBERS - 1))
        prior_spread = jnp.sqrt(jnp.sum(prior * prior, axis=0, keepdims=True) / (MEMBERS - 1))
        posterior_spread = jnp.sqrt(
            jnp.sum(posterior * posterior, axis=0, keepdims=True) / (MEMBERS - 1) + 1e-06
        )
        out[own] = posterior * (0.7 * prior_spread / posterior_spread + 0.3)


HBM = pl.BlockSpec(memory_space=pltpu.HBM)
ANY = pl.BlockSpec(memory_space=pl.ANY)
SMEM = pl.BlockSpec(memory_space=pltpu.SMEM)
VMEM = pl.BlockSpec(memory_space=pltpu.VMEM)
TOTAL = jax.ShapeDtypeStruct((9, MEMBERS, BLOCK), F32)
SIDE = jax.ShapeDtypeStruct((2, 2, REACH, MEMBERS, BLOCK), BF16)


def called(kernel, name, specs, out_shape, out_specs, scratch, pairs):
    return pl.pallas_call(
        kernel,
        in_specs=specs,
        out_shape=out_shape,
        out_specs=out_specs,
        scratch_shapes=scratch,
        compiler_params=pltpu.CompilerParams(vmem_limit_bytes=VMEM_LIMIT),
        cost_estimate=pl.CostEstimate(
            flops=pairs * 16 * MEMBERS * BLOCK * BLOCK, bytes_accessed=4 * 2**20, transcendentals=0
        ),
        name=name,
    )


def local(
    anomalies, innovations, taper_table, pair_own, pair_window, pair_taper, pair_owner, pair_count
):
    def flat(value):
        return value.reshape(8, MEMBERS, BLOCK)

    def flat_side(value):
        return value.reshape(2, 4, MEMBERS, BLOCK)

    def sides_of(anom, innov, after, count):
        return called(
            side_kernel,
            "sides",
            [ANY] * 3,
            (SIDE,) * count,
            (ANY,) * count,
            [pltpu.SemaphoreType.DMA((2 * count,))],
            0,
        )(anom, innov, after)

    partner = [permuted(v, to_partner) for v in (anomalies, innovations)]
    entries = slot_entries(
        pair_own.reshape(-1),
        pair_window.reshape(-1),
        pair_taper.reshape(-1),
        pair_count.reshape(()),
    )
    inner, outer = sides_of(anomalies, innovations, entries, 2)
    partner_outer = permuted(outer, to_diagonal)
    home_inner = permuted(inner, to_other_core)
    beyond_outer = permuted(outer, to_far_diagonal)
    beyond = [permuted(v, to_beyond) for v in partner]
    inner, outer = sides_of(*partner, entries, 2)
    home_outer = permuted(outer, to_diagonal)
    partner_inner = permuted(inner, to_other_core)

    home = flat(anomalies)
    held = [pltpu.VMEM((UNROLL, BLOCK, BLOCK), BF16)] * 2
    scratch = lambda count: [pltpu.VMEM((count, MEMBERS, BLOCK), BF16)] * 2 + held

    total, lists = called(
        first_kernel,
        "home_pairs",
        [SMEM, HBM, HBM, HBM],
        (TOTAL, jax.ShapeDtypeStruct((COUNTS + PHASES,), jnp.int32)),
        (VMEM, SMEM),
        held
        + [pltpu.VMEM((8, MEMBERS, BLOCK), BF16)] * 2
        + [pltpu.VMEM(taper_table.shape, BF16), pltpu.SemaphoreType.DMA((3,))],
        56,
    )(entries, home, flat(innovations), taper_table)
    def more(phase, name, pairs, centers, sides):
        parts = [flat(v) for v in centers] + [flat_side(v) for v in sides]
        return called(
            functools.partial(middle_kernel, phase, bool(centers)),
            name,
            [SMEM] + [VMEM] * (2 + len(parts)),
            TOTAL,
            VMEM,
            scratch(4 * len(centers) + 4 * len(sides)),
            pairs,
        )(lists, home, taper_table, *parts)

    totals = [total]
    totals.append(more(1, "partner_pairs", 63, partner, [home_inner, partner_outer]))
    totals.append(more(2, "side_pairs", 30, [], [partner_inner, home_outer, beyond_outer]))
    beyond_inner = permuted(sides_of(*beyond, totals[2], 1)[0], to_other_core)
    totals.append(more(3, "beyond_pairs", 42, beyond, []))
    out = called(
        last_kernel,
        "inflation",
        [SMEM] + [VMEM] * 7,
        jax.ShapeDtypeStruct((8, MEMBERS, BLOCK), F32),
        VMEM,
        [pltpu.VMEM(TOTAL.shape, F32)] + scratch(4),
        9,
    )(lists, home, taper_table, flat_side(beyond_inner), *totals)
    return out.reshape(anomalies.shape)


def solution(mesh):
    placed = (
        P("lat", "lon", None, None),
        P("lat", "lon", None, None),
        P(),
        P("lat", "lon", None),
        P("lat", "lon", None),
        P("lat", "lon", None),
        P("lat", "lon", None),
        P("lat", "lon"),
    )
    return jax.shard_map(
        local, mesh=mesh, in_specs=placed, out_specs=P("lat", "lon", None, None), check_vma=False
    )
```

```python
import functools

import jax
import jax.numpy as jnp
from jax import lax
from jax.experimental import pallas as pl
from jax.experimental.pallas import tpu as pltpu
from jax.sharding import PartitionSpec as P

MEMBERS = 64
BLOCK = 256
REACH = 2
UNROLL = 4
LIST = 264
SLOTS = 200
PHASES = 3
COUNTS = (PHASES + 1) * LIST
VMEM_LIMIT = 8 * 2**20
F32 = jnp.float32
BF16 = jnp.bfloat16


def permuted(value, target):
    bands, lons = (lax.axis_size("lat"), lax.axis_size("lon"))
    pairs = []
    for i in range(bands):
        for j in range(lons):
            a, b = target(i, j)
            pairs.append((i * lons + j, a * lons + b % lons))
    return lax.ppermute(value, ("lat", "lon"), pairs)


def to_partner(i, j):
    return (i ^ 1, j)


def to_beyond(i, j):
    last = lax.axis_size("lat") - 1
    target = i + 2 if i % 2 == 0 else i - 2
    return (target if 0 <= target <= last else i ^ 1, j)


def to_far_diagonal(i, j):
    last = lax.axis_size("lat") - 1
    target = i + 1 if i % 2 else i - 1
    return (target if 0 <= target <= last else i, j + 1 if j % 2 else j - 1)


def to_diagonal(i, j):
    return (i ^ 1, j + 1 if j % 2 else j - 1)


def to_other_core(i, j):
    return (i, j ^ 1)


def slot_entries(own, window, taper, count):
    row, lon = (window // 8, window % 8)
    odd_lat = lax.axis_index("lat") % 2
    odd_lon = lax.axis_index("lon") % 2
    partner_row = jnp.where(odd_lat == 1, 0, 2)
    rows = row // 2
    group = jnp.where(rows == 1, 0, jnp.where(rows == partner_row, 1, 2))
    west = lon < REACH
    east = lon >= 8 - REACH
    outer = jnp.where(odd_lon == 1, east, west)
    side = west | east
    center_slot = jnp.where(group == 1, 8, 0) + (row % 2) * 4 + lon - REACH
    side_slot = (row % 2) * 2 + jnp.where(west, lon, lon - 6)
    late = ~outer | (group == 0)
    phase = jnp.where(side, jnp.where(late, 2, 1), group // 2)
    outer_slot = jnp.where(group == 1, 8, 12)
    slot = jnp.where(side, jnp.where(outer, outer_slot, group * 4) + side_slot, center_slot)
    live = jnp.arange(SLOTS, dtype=jnp.int32) < count
    phase = jnp.where(live, phase, PHASES)
    padding = jnp.arange(LIST - SLOTS, dtype=jnp.int32)
    entries = jnp.concatenate(
        [own + slot * 16 + (taper + 8) % 16 * 1024, jnp.full((LIST - SLOTS,), 8, jnp.int32)]
    )
    phases = jnp.concatenate([phase, jnp.minimum(padding // (3 * UNROLL), PHASES)])
    index = jnp.arange(LIST, dtype=jnp.int32)
    earlier = (phases[:, None] == phases[None, :]) & (index[:, None] < index[None, :])
    place = jnp.sum(earlier.astype(jnp.int32), axis=0)
    return entries + (phases * LIST + place) * 16384


def pairs_of(lists, phase, home, window_anom, window_innov, tapers, total, even, odd):
    def entry_at(group, lane):
        return lists[phase * LIST + group * UNROLL + lane]

    def tiles(group, kept):
        for lane in range(UNROLL):
            entry = entry_at(group, lane)
            product = lax.dot_general(
                window_anom[(entry >> 4) & 63],
                home[entry & 7],
                (((0,), (0,)), ((), ())),
                preferred_element_type=F32,
            )
            kept[lane] = (product * tapers[(entry >> 10) & 15].astype(F32)).astype(BF16)

    def increments(group, kept):
        for lane in range(UNROLL):
            entry = entry_at(group, lane)
            total[entry & 15] += jnp.dot(
                window_innov[(entry >> 4) & 63], kept[lane], preferred_element_type=F32
            )

    def two_groups(step, carry):
        tiles(2 * step + 1, odd)
        increments(2 * step, even)
        tiles(2 * step + 2, even)
        increments(2 * step + 1, odd)
        return carry

    tiles(0, even)
    groups = (lists[COUNTS + phase] + UNROLL - 1) // UNROLL
    lax.fori_loop(0, (groups + 1) // 2, two_groups, 0)


def copied(pairs, done):
    copies = [
        pltpu.make_async_copy(source, target, done.at[i])
        for i, (source, target) in enumerate(pairs)
    ]
    for copy in copies:
        copy.start()
    for copy in copies:
        copy.wait()


def load_kernel(anom, innov, table, after, home, home_innov, tapers, outer, done):
    columns = pl.ds(2 * (lax.axis_index("lon") % 2), REACH)
    pairs = [(anom, home), (innov, home_innov)]
    pairs += [(v.at[:, columns], outer.at[i]) for i, v in enumerate((anom, innov))]
    pairs += [(table.at[4 * i : 4 * i + 4], tapers.at[4 * i : 4 * i + 4]) for i in range(4)]
    copied(pairs, done)


def outer_kernel(anom, innov, side, done):
    columns = pl.ds(2 * (lax.axis_index("lon") % 2), REACH)
    copied([(v.at[:, columns], side.at[i]) for i, v in enumerate((anom, innov))], done)


def inner_kernel(near, anom, innov, *refs):
    side, done = refs[-2:]
    columns = pl.ds(2 - 2 * (lax.axis_index("lon") % 2), REACH)
    pairs = [(near.at[i], side.at[i, 0:4]) for i in range(2)]
    pairs += [(v.at[:, columns], side.at[i, 4:6]) for i, v in enumerate((anom, innov))]
    copied(pairs, done)


def near_kernel(entries, home, home_innov, tapers, partner, partner_innov, *refs):
    total, lists, near, anom, innov, even, odd = refs
    anom[0:8] = home[...]
    anom[8:16] = partner[...]
    innov[0:8] = home_innov[...]
    innov[8:16] = partner_innov[...]
    first = 2 - 2 * (lax.axis_index("lon") % 2)
    for row in range(4):
        near[0, row] = anom[pl.ds(row * 4 + first, REACH)]
        near[1, row] = innov[pl.ds(row * 4 + first, REACH)]

    def place(step, carry):
        for lane in range(8):
            entry = entries[step * 8 + lane]
            lists[entry >> 14] = entry & 16383
        return carry

    lax.fori_loop(0, LIST // 8, place, 0)
    for phase in range(PHASES):
        first = entries[SLOTS + 3 * UNROLL * phase] >> 14
        lists[COUNTS + phase] = first - phase * LIST
    total[...] = jnp.zeros_like(total)
    pairs_of(lists, 0, anom, anom, innov, tapers, total, even, odd)


def gathered(centers, sides, anom, innov):
    anom[0:8] = centers[0][...]
    innov[0:8] = centers[1][...]
    for i, side in enumerate(sides):
        anom[8 + 4 * i : 12 + 4 * i] = side[0]
        innov[8 + 4 * i : 12 + 4 * i] = side[1]


def middle_kernel(phase, lists, home, tapers, *rest):
    parts, (total, anom, innov, even, odd) = (rest[:-5], rest[-5:])
    gathered(parts[:2], parts[2:], anom, innov)
    total[...] = jnp.zeros_like(total)
    pairs_of(lists, phase, home, anom, innov, tapers, total, even, odd)


def last_kernel(lists, home, tapers, inner, outer, *rest):
    before, (out, total, anom, innov, even, odd) = (rest[:-6], rest[-6:])
    for part, blocks in enumerate((anom, innov)):
        blocks[0:12] = inner[part]
        blocks[12:16] = outer[part]
    total[...] = jnp.zeros_like(total)
    pairs_of(lists, 2, home, anom, innov, tapers, total, even, odd)
    for own in range(8):
        prior = home[own].astype(F32)
        increment = total[own]
        for part in before:
            increment += part[own]
        posterior = prior - increment * (1.0 / (MEMBERS - 1))
        prior_spread = jnp.sqrt(jnp.sum(prior * prior, axis=0, keepdims=True) / (MEMBERS - 1))
        posterior_spread = jnp.sqrt(
            jnp.sum(posterior * posterior, axis=0, keepdims=True) / (MEMBERS - 1) + 1e-06
        )
        out[own] = posterior * (0.7 * prior_spread / posterior_spread + 0.3)


ANY = pl.BlockSpec(memory_space=pl.ANY)
SMEM = pl.BlockSpec(memory_space=pltpu.SMEM)
VMEM = pl.BlockSpec(memory_space=pltpu.VMEM)
TOTAL = jax.ShapeDtypeStruct((9, MEMBERS, BLOCK), F32)


def called(kernel, name, specs, out_shape, out_specs, scratch, pairs):
    return pl.pallas_call(
        kernel,
        in_specs=specs,
        out_shape=out_shape,
        out_specs=out_specs,
        scratch_shapes=scratch,
        compiler_params=pltpu.CompilerParams(vmem_limit_bytes=VMEM_LIMIT),
        cost_estimate=pl.CostEstimate(
            flops=pairs * 16 * MEMBERS * BLOCK * BLOCK, bytes_accessed=4 * 2**20, transcendentals=0
        ),
        name=name,
    )


def local(
    anomalies, innovations, taper_table, pair_own, pair_window, pair_taper, pair_owner, pair_count
):
    def flat(value):
        return value.reshape(8, MEMBERS, BLOCK)

    def flat_side(value):
        return value.reshape(2, -1, MEMBERS, BLOCK)

    partner = [permuted(v, to_partner) for v in (anomalies, innovations)]
    entries = slot_entries(
        pair_own.reshape(-1),
        pair_window.reshape(-1),
        pair_taper.reshape(-1),
        pair_count.reshape(()),
    )
    row = jax.ShapeDtypeStruct(anomalies.shape, BF16)
    anomalies, innovations, taper_table, outer = called(
        load_kernel,
        "load",
        [ANY] * 4,
        (
            row,
            row,
            jax.ShapeDtypeStruct(taper_table.shape, BF16),
            jax.ShapeDtypeStruct((2, 2, REACH, MEMBERS, BLOCK), BF16),
        ),
        (VMEM,) * 4,
        [pltpu.SemaphoreType.DMA((8,))],
        0,
    )(anomalies, innovations, taper_table, entries)
    partner_outer = permuted(outer, to_diagonal)
    beyond_outer = permuted(outer, to_far_diagonal)
    beyond = [permuted(v, to_beyond) for v in partner]
    partner_cut = called(
        outer_kernel,
        "outer_sides",
        [ANY] * 2,
        jax.ShapeDtypeStruct(outer.shape, BF16),
        ANY,
        [pltpu.SemaphoreType.DMA((2,))],
        0,
    )(*partner)
    home_outer = permuted(partner_cut, to_diagonal)
    home = flat(anomalies)
    held = [pltpu.VMEM((UNROLL, BLOCK, BLOCK), BF16)] * 2

    def blocks(count):
        return [pltpu.VMEM((count, MEMBERS, BLOCK), BF16)] * 2 + held

    near_total, lists, near = called(
        near_kernel,
        "near_pairs",
        [SMEM] + [VMEM] * 5,
        (
            TOTAL,
            jax.ShapeDtypeStruct((COUNTS + PHASES,), jnp.int32),
            jax.ShapeDtypeStruct((2, 4, REACH, MEMBERS, BLOCK), BF16),
        ),
        (VMEM, SMEM, VMEM),
        blocks(16),
        98,
    )(entries, home, flat(innovations), taper_table, flat(partner[0]), flat(partner[1]))
    inner = permuted(
        called(
            inner_kernel,
            "inner_sides",
            [ANY] * 6,
            jax.ShapeDtypeStruct((2, 6, REACH, MEMBERS, BLOCK), BF16),
            ANY,
            [pltpu.SemaphoreType.DMA((4,))],
            0,
        )(near, *beyond, home_outer, partner_outer, beyond_outer),
        to_other_core,
    )
    beyond_total = called(
        functools.partial(middle_kernel, 1),
        "beyond_pairs",
        [SMEM] + [VMEM] * 6,
        TOTAL,
        VMEM,
        blocks(16),
        60,
    )(
        lists,
        home,
        taper_table,
        flat(beyond[0]),
        flat(beyond[1]),
        flat_side(partner_outer),
        flat_side(beyond_outer),
    )
    totals = [near_total, beyond_total]
    out = called(
        last_kernel,
        "inflation",
        [SMEM] + [VMEM] * 6,
        jax.ShapeDtypeStruct((8, MEMBERS, BLOCK), F32),
        VMEM,
        [pltpu.VMEM(TOTAL.shape, F32)] + [pltpu.VMEM((16, MEMBERS, BLOCK), BF16)] * 2 + held,
        42,
    )(lists, home, taper_table, flat_side(inner), flat_side(home_outer), *totals)
    return out.reshape(anomalies.shape)


def solution(mesh):
    placed = (
        P("lat", "lon", None, None),
        P("lat", "lon", None, None),
        P(),
        P("lat", "lon", None),
        P("lat", "lon", None),
        P("lat", "lon", None),
        P("lat", "lon", None),
        P("lat", "lon"),
    )
    return jax.shard_map(
        local, mesh=mesh, in_specs=placed, out_specs=P("lat", "lon", None, None), check_vma=False
    )
```

```python
import functools

import jax
import jax.numpy as jnp
from jax import lax
from jax.experimental import pallas as pl
from jax.experimental.pallas import tpu as pltpu
from jax.sharding import PartitionSpec as P

MEMBERS = 64
BLOCK = 256
REACH = 2
UNROLL = 4
LIST = 264
SLOTS = 200
PHASES = 3
COUNTS = (PHASES + 1) * LIST
VMEM_LIMIT = 8 * 2**20
F32 = jnp.float32
BF16 = jnp.bfloat16


def permuted(value, target):
    bands, lons = (lax.axis_size("lat"), lax.axis_size("lon"))
    pairs = []
    for i in range(bands):
        for j in range(lons):
            a, b = target(i, j)
            pairs.append((i * lons + j, a * lons + b % lons))
    return lax.ppermute(value, ("lat", "lon"), pairs)


def to_partner(i, j):
    return (i ^ 1, j)


def to_beyond(i, j):
    last = lax.axis_size("lat") - 1
    target = i + 2 if i % 2 == 0 else i - 2
    return (target if 0 <= target <= last else i ^ 1, j)


def to_far_diagonal(i, j):
    last = lax.axis_size("lat") - 1
    target = i + 1 if i % 2 else i - 1
    return (target if 0 <= target <= last else i, j + 1 if j % 2 else j - 1)


def to_diagonal(i, j):
    return (i ^ 1, j + 1 if j % 2 else j - 1)


def to_other_core(i, j):
    return (i, j ^ 1)


def slot_entries(own, window, taper, count):
    row, lon = (window // 8, window % 8)
    odd_lat = lax.axis_index("lat") % 2
    odd_lon = lax.axis_index("lon") % 2
    partner_row = jnp.where(odd_lat == 1, 0, 2)
    rows = row // 2
    group = jnp.where(rows == 1, 0, jnp.where(rows == partner_row, 1, 2))
    west = lon < REACH
    east = lon >= 8 - REACH
    outer = jnp.where(odd_lon == 1, east, west)
    side = west | east
    center_slot = jnp.where(group == 1, 8, 0) + (row % 2) * 4 + lon - REACH
    side_slot = (row % 2) * 2 + jnp.where(west, lon, lon - 6)
    phase = jnp.where(side, jnp.where(outer, 1, 2), group // 2)
    outer_slot = jnp.where(group == 1, 8, jnp.where(group == 2, 12, 16))
    slot = jnp.where(side, jnp.where(outer, outer_slot, group * 4) + side_slot, center_slot)
    live = jnp.arange(SLOTS, dtype=jnp.int32) < count
    phase = jnp.where(live, phase, PHASES)
    padding = jnp.arange(LIST - SLOTS, dtype=jnp.int32)
    entries = jnp.concatenate(
        [own + slot * 16 + (taper + 8) % 16 * 1024, jnp.full((LIST - SLOTS,), 8, jnp.int32)]
    )
    phases = jnp.concatenate([phase, jnp.minimum(padding // (3 * UNROLL), PHASES)])
    index = jnp.arange(LIST, dtype=jnp.int32)
    earlier = (phases[:, None] == phases[None, :]) & (index[:, None] < index[None, :])
    place = jnp.sum(earlier.astype(jnp.int32), axis=0)
    return entries + (phases * LIST + place) * 16384


def pairs_of(lists, phase, home, window_anom, window_innov, tapers, total, even, odd):
    def entry_at(group, lane):
        return lists[phase * LIST + group * UNROLL + lane]

    def tiles(group, kept):
        for lane in range(UNROLL):
            entry = entry_at(group, lane)
            product = lax.dot_general(
                window_anom[(entry >> 4) & 63],
                home[entry & 7],
                (((0,), (0,)), ((), ())),
                preferred_element_type=F32,
            )
            kept[lane] = (product * tapers[(entry >> 10) & 15].astype(F32)).astype(BF16)

    def increments(group, kept):
        for lane in range(UNROLL):
            entry = entry_at(group, lane)
            total[entry & 15] += jnp.dot(
                window_innov[(entry >> 4) & 63], kept[lane], preferred_element_type=F32
            )

    def two_groups(step, carry):
        tiles(2 * step + 1, odd)
        increments(2 * step, even)
        tiles(2 * step + 2, even)
        increments(2 * step + 1, odd)
        return carry

    tiles(0, even)
    groups = (lists[COUNTS + phase] + UNROLL - 1) // UNROLL
    lax.fori_loop(0, (groups + 1) // 2, two_groups, 0)


def copied(pairs, done):
    copies = [
        pltpu.make_async_copy(source, target, done.at[i])
        for i, (source, target) in enumerate(pairs)
    ]
    for copy in copies:
        copy.start()
    for copy in copies:
        copy.wait()


def load_kernel(anom, innov, table, after, home, home_innov, tapers, outer, done):
    columns = pl.ds(2 * (lax.axis_index("lon") % 2), REACH)
    pairs = [(anom, home), (innov, home_innov)]
    pairs += [(v.at[:, columns], outer.at[i]) for i, v in enumerate((anom, innov))]
    pairs += [(table.at[4 * i : 4 * i + 4], tapers.at[4 * i : 4 * i + 4]) for i in range(4)]
    copied(pairs, done)


def outer_kernel(anom, innov, side, done):
    columns = pl.ds(2 * (lax.axis_index("lon") % 2), REACH)
    copied([(v.at[:, columns], side.at[i]) for i, v in enumerate((anom, innov))], done)


def inner_kernel(near, anom, innov, *refs):
    side, done = refs[-2:]
    columns = pl.ds(2 - 2 * (lax.axis_index("lon") % 2), REACH)
    pairs = [(near.at[i], side.at[i, 0:4]) for i in range(2)]
    pairs += [(v.at[:, columns], side.at[i, 4:6]) for i, v in enumerate((anom, innov))]
    copied(pairs, done)


def near_kernel(entries, home, home_innov, tapers, partner, partner_innov, *refs):
    total, lists, near, anom, innov, even, odd = refs
    anom[0:8] = home[...]
    anom[8:16] = partner[...]
    innov[0:8] = home_innov[...]
    innov[8:16] = partner_innov[...]
    first = 2 - 2 * (lax.axis_index("lon") % 2)
    for row in range(4):
        near[0, row] = anom[pl.ds(row * 4 + first, REACH)]
        near[1, row] = innov[pl.ds(row * 4 + first, REACH)]

    def place(step, carry):
        for lane in range(8):
            entry = entries[step * 8 + lane]
            lists[entry >> 14] = entry & 16383
        return carry

    lax.fori_loop(0, LIST // 8, place, 0)
    for phase in range(PHASES):
        first = entries[SLOTS + 3 * UNROLL * phase] >> 14
        lists[COUNTS + phase] = first - phase * LIST
    total[...] = jnp.zeros_like(total)
    pairs_of(lists, 0, anom, anom, innov, tapers, total, even, odd)


def gathered(centers, sides, anom, innov):
    anom[0:8] = centers[0][...]
    innov[0:8] = centers[1][...]
    for i, side in enumerate(sides):
        anom[8 + 4 * i : 12 + 4 * i] = side[0]
        innov[8 + 4 * i : 12 + 4 * i] = side[1]


def middle_kernel(phase, lists, home, tapers, *rest):
    parts, (total, anom, innov, even, odd) = (rest[:-5], rest[-5:])
    gathered(parts[:2], parts[2:], anom, innov)
    total[...] = jnp.zeros_like(total)
    pairs_of(lists, phase, home, anom, innov, tapers, total, even, odd)


def last_kernel(lists, home, tapers, inner, *rest):
    before, (out, total, anom, innov, even, odd) = (rest[:-6], rest[-6:])
    for part, blocks in enumerate((anom, innov)):
        blocks[0:12] = inner[part]
    total[...] = jnp.zeros_like(total)
    pairs_of(lists, 2, home, anom, innov, tapers, total, even, odd)
    for own in range(8):
        prior = home[own].astype(F32)
        increment = total[own]
        for part in before:
            increment += part[own]
        posterior = prior - increment * (1.0 / (MEMBERS - 1))
        prior_spread = jnp.sqrt(jnp.sum(prior * prior, axis=0, keepdims=True) / (MEMBERS - 1))
        posterior_spread = jnp.sqrt(
            jnp.sum(posterior * posterior, axis=0, keepdims=True) / (MEMBERS - 1) + 1e-06
        )
        out[own] = posterior * (0.7 * prior_spread / posterior_spread + 0.3)


ANY = pl.BlockSpec(memory_space=pl.ANY)
SMEM = pl.BlockSpec(memory_space=pltpu.SMEM)
VMEM = pl.BlockSpec(memory_space=pltpu.VMEM)
TOTAL = jax.ShapeDtypeStruct((9, MEMBERS, BLOCK), F32)


def called(kernel, name, specs, out_shape, out_specs, scratch, pairs):
    return pl.pallas_call(
        kernel,
        in_specs=specs,
        out_shape=out_shape,
        out_specs=out_specs,
        scratch_shapes=scratch,
        compiler_params=pltpu.CompilerParams(vmem_limit_bytes=VMEM_LIMIT),
        cost_estimate=pl.CostEstimate(
            flops=pairs * 16 * MEMBERS * BLOCK * BLOCK, bytes_accessed=4 * 2**20, transcendentals=0
        ),
        name=name,
    )


def local(
    anomalies, innovations, taper_table, pair_own, pair_window, pair_taper, pair_owner, pair_count
):
    def flat(value):
        return value.reshape(8, MEMBERS, BLOCK)

    def flat_side(value):
        return value.reshape(2, -1, MEMBERS, BLOCK)

    partner = [permuted(v, to_partner) for v in (anomalies, innovations)]
    entries = slot_entries(
        pair_own.reshape(-1),
        pair_window.reshape(-1),
        pair_taper.reshape(-1),
        pair_count.reshape(()),
    )
    row = jax.ShapeDtypeStruct(anomalies.shape, BF16)
    anomalies, innovations, taper_table, outer = called(
        load_kernel,
        "load",
        [ANY] * 4,
        (
            row,
            row,
            jax.ShapeDtypeStruct(taper_table.shape, BF16),
            jax.ShapeDtypeStruct((2, 2, REACH, MEMBERS, BLOCK), BF16),
        ),
        (VMEM,) * 4,
        [pltpu.SemaphoreType.DMA((8,))],
        0,
    )(anomalies, innovations, taper_table, entries)
    partner_outer = permuted(outer, to_diagonal)
    beyond_outer = permuted(outer, to_far_diagonal)
    beyond = [permuted(v, to_beyond) for v in partner]
    partner_cut = called(
        outer_kernel,
        "outer_sides",
        [ANY] * 2,
        jax.ShapeDtypeStruct(outer.shape, BF16),
        ANY,
        [pltpu.SemaphoreType.DMA((2,))],
        0,
    )(*partner)
    home_outer = permuted(partner_cut, to_diagonal)
    home = flat(anomalies)
    held = [pltpu.VMEM((UNROLL, BLOCK, BLOCK), BF16)] * 2

    def blocks(count):
        return [pltpu.VMEM((count, MEMBERS, BLOCK), BF16)] * 2 + held

    near_total, lists, near = called(
        near_kernel,
        "near_pairs",
        [SMEM] + [VMEM] * 5,
        (
            TOTAL,
            jax.ShapeDtypeStruct((COUNTS + PHASES,), jnp.int32),
            jax.ShapeDtypeStruct((2, 4, REACH, MEMBERS, BLOCK), BF16),
        ),
        (VMEM, SMEM, VMEM),
        blocks(16),
        98,
    )(entries, home, flat(innovations), taper_table, flat(partner[0]), flat(partner[1]))
    inner = permuted(
        called(
            inner_kernel,
            "inner_sides",
            [ANY] * 6,
            jax.ShapeDtypeStruct((2, 6, REACH, MEMBERS, BLOCK), BF16),
            ANY,
            [pltpu.SemaphoreType.DMA((4,))],
            0,
        )(near, *beyond, home_outer, partner_outer, beyond_outer),
        to_other_core,
    )
    beyond_total = called(
        functools.partial(middle_kernel, 1),
        "beyond_pairs",
        [SMEM] + [VMEM] * 7,
        TOTAL,
        VMEM,
        blocks(20),
        72,
    )(
        lists,
        home,
        taper_table,
        flat(beyond[0]),
        flat(beyond[1]),
        flat_side(partner_outer),
        flat_side(beyond_outer),
        flat_side(home_outer),
    )
    totals = [near_total, beyond_total]
    out = called(
        last_kernel,
        "inflation",
        [SMEM] + [VMEM] * 5,
        jax.ShapeDtypeStruct((8, MEMBERS, BLOCK), F32),
        VMEM,
        [pltpu.VMEM(TOTAL.shape, F32)] + [pltpu.VMEM((12, MEMBERS, BLOCK), BF16)] * 2 + held,
        30,
    )(lists, home, taper_table, flat_side(inner), *totals)
    return out.reshape(anomalies.shape)


def solution(mesh):
    placed = (
        P("lat", "lon", None, None),
        P("lat", "lon", None, None),
        P(),
        P("lat", "lon", None),
        P("lat", "lon", None),
        P("lat", "lon", None),
        P("lat", "lon", None),
        P("lat", "lon"),
    )
    return jax.shard_map(
        local, mesh=mesh, in_specs=placed, out_specs=P("lat", "lon", None, None), check_vma=False
    )
```
